256 devices in a mesh: dp: 16 (over y_lo, z), tensor: 16 (over x, y_hi, core).
Axes of the slice: x: 4, y: 4 (y_hi: 2, y_lo: 2; y = y_hi * 2 + y_lo), z: 8, core: 2. Of those that a mesh axis runs over, the one named last changes fastest.
Arguments:
- tokens: bfloat16 [2048, 6144], P('dp', 'tensor'), may hold values from -6 to 6
- cotangent: bfloat16 [2048, 6144], P('dp', 'tensor'), may hold values from -6 to 6
- up_blocks: bfloat16 [96, 4, 256, 256], P('tensor'), may hold values from -0.1875 to 0.1875
- up_index: int32 [96, 4], P('tensor'), may hold values from 0 to 23, all different within a row
- down_blocks: bfloat16 [96, 4, 256, 256], P('tensor'), may hold values from -0.09375 to 0.09375
- down_index: int32 [96, 4], P('tensor'), may hold values from 0 to 23, all different within a row
Outputs:
- output: bfloat16 [2048, 6144], P('dp', 'tensor')
- input_grad: bfloat16 [2048, 6144], P('dp', 'tensor')
- up_grad: bfloat16 [96, 4, 256, 256], P('tensor', None, 'dp')
- down_grad: bfloat16 [96, 4, 256, 256], P('tensor', None, 'dp')
The draws below stay inside these ranges and needn't reach their ends.
Inputs may be any that keep to these rules, and one draw needn't show every extreme that they name: `up_index`: each row names 4 different feature blocks; every one of the 24 feature blocks is named by some row. `down_index`: each row names 4 different feature blocks; every one of the 24 feature blocks is named by some row.
All inputs are finite; a program needn't handle non-finite values.
Results may differ from the reference program's by a relative error of at most 0.022.
Values may be sent and summed in bfloat16 or wider, within the bound.
No kernel may reach another device: no remote copies, remote signals or barrier semaphores. Data moves between devices by JAX's collectives and lax.ppermute only.
A program may use at most 64 MiB of HBM per device.

```python
import jax
import jax.numpy as jnp
from jax import lax

D = 6144
BLK = 256
K = 4
TOK_DEV = 128
DB = 24
HB = 96
HB_DEV = 6
TOKENS = 2048
N_DP = 16
N_TENSOR = 16


def steps_of(rng, shape, split, smallest, high):
    gain = 1.0
    for position, blocks in split:
        steps = jax.random.uniform(jax.random.fold_in(jax.random.fold_in(rng, 6), position), (blocks,), jnp.float32, smallest / len(split), high / len(split))
        gain = gain * jnp.repeat(jnp.exp(steps), shape[position] // blocks).reshape((-1,) + (1,) * (len(shape) - 1 - position))
    return gain


def choose_distinct(key, rows, number_of, top, lift):
    order = jax.random.permutation(jax.random.fold_in(key, 1), number_of)
    pull = order
    for power in range(3):
        pull = pull * pull // number_of
    pull = pull * lift // number_of
    tickets = jax.random.randint(jax.random.fold_in(key, 2), (rows, number_of), 0, 4096) + pull
    fixed_rows = jax.random.permutation(jax.random.fold_in(key, 3), rows)[jnp.arange(number_of) % rows]
    tickets = jnp.where(jnp.arange(rows)[:, None] == fixed_rows[None, :], 1 << 14, tickets)
    score = tickets * number_of + jnp.arange(number_of)
    return lax.top_k(score.astype(jnp.int32), top)[1].astype(jnp.int32)


def scatter_about(own_key, extent, spread, reach, shards=(), kind=jnp.bfloat16):
    array = jax.random.normal(own_key, extent, jnp.float32) * spread
    if len(shards) > 0:
        array = steps_of(own_key, extent, shards, -0.22, 0.18) * array
    return jnp.clip(array, min=-reach, max=reach).astype(kind)


def setup_inputs(seed: int = 0) -> dict:
    streams_of = jax.random.split(jax.random.key(seed), 7)
    tokens = scatter_about(streams_of[0], (TOKENS, D), 1.0, 6.0, ((0, 16), (1, 16)))
    cotangent = scatter_about(streams_of[1], (TOKENS, D), 1.0, 6.0, ((0, 16), (1, 16)))
    up_blocks = scatter_about(streams_of[2], (HB, K, BLK, BLK), (K * BLK) ** -0.5, 0.1875, ((0, 16),))
    up_index = choose_distinct(streams_of[3], HB, DB, K, 0)
    down_blocks = scatter_about(streams_of[4], (HB, K, BLK, BLK), (HB * K * BLK // DB) ** -0.5, 0.09375, ((0, 16),))
    down_index = choose_distinct(streams_of[5], HB, DB, K, 0)
    return {"tokens": tokens, "cotangent": cotangent, "up_blocks": up_blocks, "up_index": up_index, "down_blocks": down_blocks, "down_index": down_index}


def pick_blocks(rows, index_table):
    blocked = rows.reshape(rows.shape[0], DB, BLK)
    picked = jnp.take(blocked, index_table.reshape(-1).astype(jnp.int32), axis=1)
    return picked.reshape(rows.shape[0], HB, K, BLK)


def group_sums(partial_terms, index_table):
    row_count = partial_terms.shape[0]
    grouped = partial_terms.reshape(row_count, N_TENSOR, HB_DEV * K, BLK)
    labels = index_table.reshape(N_TENSOR, HB_DEV * K)
    one_hot = (labels[:, :, None] == jnp.arange(DB, dtype=jnp.int32)[None, None, :]).astype(jnp.float32)
    placed = jnp.einsum("tgjd,gjb->tgbd", grouped, one_hot, precision=lax.Precision.HIGHEST)
    rounded = lax.optimization_barrier(placed.astype(jnp.bfloat16)).astype(jnp.float32)
    return jnp.sum(rounded, axis=1).reshape(row_count, D)


def reference(tokens, cotangent, up_blocks, up_index, down_blocks, down_index):
    highest = lax.Precision.HIGHEST
    up_wide = up_blocks.astype(jnp.float32)
    down_wide = down_blocks.astype(jnp.float32)

    def shard_pass(carry, inputs):
        up_total, down_total = carry
        token_rows, grad_rows = inputs
        picked = pick_blocks(token_rows, up_index).astype(jnp.float32)
        pre_act = jnp.einsum("tnki,nkio->tno", picked, up_wide, precision=highest)
        hidden = jax.nn.silu(pre_act).astype(jnp.bfloat16)
        hidden_wide = hidden.astype(jnp.float32)
        out_terms = jnp.einsum("tno,nkod->tnkd", hidden_wide, down_wide, precision=highest)
        output = group_sums(out_terms, down_index).astype(jnp.bfloat16)
        grad_picked = pick_blocks(grad_rows, down_index).astype(jnp.float32)
        grad_hidden = jnp.einsum("tnkd,nkod->tno", grad_picked, down_wide, precision=highest)
        sigmoid_val = jax.nn.sigmoid(pre_act)
        slope = sigmoid_val * (1.0 + pre_act * (1.0 - sigmoid_val))
        pre_grad = (grad_hidden * slope).astype(jnp.bfloat16)
        pre_wide = pre_grad.astype(jnp.float32)
        in_terms = jnp.einsum("tno,nkio->tnki", pre_wide, up_wide, precision=highest)
        input_grad = group_sums(in_terms, up_index).astype(jnp.bfloat16)
        up_part = jnp.einsum("tnki,tno->nkio", picked, pre_wide, precision=highest)
        down_part = jnp.einsum("tno,tnkd->nkod", hidden_wide, grad_picked, precision=highest)
        up_total = up_total + lax.optimization_barrier(up_part.astype(jnp.bfloat16)).astype(jnp.float32)
        down_total = down_total + lax.optimization_barrier(down_part.astype(jnp.bfloat16)).astype(jnp.float32)
        return (up_total, down_total), (output, input_grad)

    start = (jnp.zeros((HB, K, BLK, BLK), jnp.float32), jnp.zeros((HB, K, BLK, BLK), jnp.float32))
    token_shards = tokens.reshape(N_DP, TOK_DEV, D)
    grad_shards = cotangent.reshape(N_DP, TOK_DEV, D)
    (up_total, down_total), (outputs, input_grads) = lax.scan(shard_pass, start, (token_shards, grad_shards))
    output = outputs.reshape(TOKENS, D)
    input_grad = input_grads.reshape(TOKENS, D)
    return (output, input_grad, up_total.astype(jnp.bfloat16), down_total.astype(jnp.bfloat16))
```

```python
import jax
import jax.numpy as jnp
from jax import lax
from jax.experimental import pallas as pl
from jax.experimental.pallas import tpu as pltpu
from jax.sharding import Mesh, PartitionSpec as P

BLK = 256
HALF = 128
WIDE = 384
K = 4
NL = 3
AXES = ("ylo", "z", "x", "yhi", "core")
VMEM_LIMIT = 48 * 1024 * 1024


def device_id(x, y, z, c):
    return ((y % 2) * 8 + z) * 16 + x * 4 + (y // 2) * 2 + c


def permute(value, target):
    pairs = []
    for x in range(4):
        for y in range(4):
            for z in range(8):
                for c in range(2):
                    tx, ty, tc = target(x, y, c)
                    pairs.append((device_id(x, y, z, c), device_id(tx % 4, ty % 4, z, tc)))
    return lax.ppermute(value, AXES, pairs)


def other_core(x, y, c):
    return x, y, 1 - c


def other_half(x, y, c):
    return x, y ^ 1, c


def first_axis(step):
    return lambda x, y, c: (x + step, y, c) if c == 0 else (x, y + step, c)


def second_axis(step):
    return lambda x, y, c: (x, y + step, c) if c == 0 else (x + step, y, c)


def piece_tables(index_table, x, y, kind, sign):
    unit = index_table.reshape(-1)[:, None] * 2 + jnp.arange(2, dtype=jnp.int32)[None, :]
    owner = unit // 3
    lane = (unit % 3) * HALF
    px = owner // 4
    py = ((owner // 2) % 2)[:, :, None] * 2 + jnp.arange(2, dtype=jnp.int32)
    dx = ((sign * (px - x)) % 4)[:, :, None] + jnp.zeros_like(py)
    dy = (sign * (py - y)) % 4
    slot = ((owner % 2) ^ kind)[:, :, None]
    return dx, dy, slot, lane


def grads_kernel(tab_ref, tok_lane, cot_lane, tok_piece, cot_piece, *refs):
    mine, theirs = refs[0:4], refs[4:8]
    up_ref, down_ref, hid_ref, pg_ref, dw_ref = refs[8:13]
    toks, cots, ups, downs, sem = refs[13:]
    core, half = tab_ref[0], tab_ref[1]
    up_copy = pltpu.make_async_copy(up_ref.at[pl.ds(half * NL, NL)], ups, sem.at[0])
    down_copy = pltpu.make_async_copy(down_ref.at[pl.ds(half * NL, NL)], downs, sem.at[1])
    up_copy.start()

    @pl.when(core == 0)
    def _():
        for e in range(4):
            pltpu.make_async_copy(mine[e], toks.at[e], sem.at[2]).start()

    @pl.when(core == 1)
    def _():
        for e in range(4):
            pltpu.make_async_copy(theirs[e], toks.at[e], sem.at[2]).start()

    down_copy.start()

    @pl.when(core == 0)
    def _():
        for e in range(4):
            pltpu.make_async_copy(theirs[e], cots.at[e], sem.at[3]).start()

    @pl.when(core == 1)
    def _():
        for e in range(4):
            pltpu.make_async_copy(mine[e], cots.at[e], sem.at[3]).start()

    def block(ref, piece, lane, j):
        rows = []
        for h in range(2):
            cols = []
            for u in range(2):
                p = piece[(j * 2 + u) * 2 + h]
                off = pl.multiple_of(lane[j * 2 + u], HALF)
                cols.append(ref[p // 8, (p // 2) % 4, p % 2, :, pl.ds(off, HALF)])
            rows.append(jnp.concatenate(cols, axis=1))
        return jnp.concatenate(rows, axis=0)

    def store(grad, j, value):
        value = value.astype(jnp.bfloat16)
        for d in range(16):
            dw_ref[d % 8, d // 8, grad, j] = value[d * 16 : d * 16 + 16]

    up_copy.wait()
    pltpu.make_async_copy(toks, toks, sem.at[2]).wait()
    pres = []
    for n in range(NL):
        acc = jnp.zeros((BLK, BLK), jnp.float32)
        for k in range(K):
            acc += jnp.dot(
                block(toks, tok_piece, tok_lane, n * K + k),
                ups[n, k],
                preferred_element_type=jnp.float32,
            )
        pres.append(acc)
        hid_ref[n] = (acc * jax.nn.sigmoid(acc)).astype(jnp.bfloat16)
    down_copy.wait()
    pltpu.make_async_copy(cots, cots, sem.at[3]).wait()
    for n in range(NL):
        acc = jnp.zeros((BLK, BLK), jnp.float32)
        hidden = hid_ref[n]
        for k in range(K):
            cot = block(cots, cot_piece, cot_lane, n * K + k)
            acc += lax.dot_general(
                cot, downs[n, k], (((1,), (1,)), ((), ())), preferred_element_type=jnp.float32
            )
            store(
                1,
                n * K + k,
                lax.dot_general(
                    hidden, cot, (((0,), (0,)), ((), ())), preferred_element_type=jnp.float32
                ),
            )
        sig = jax.nn.sigmoid(pres[n])
        pg_ref[n] = (acc * (sig * (1.0 + pres[n] * (1.0 - sig)))).astype(jnp.bfloat16)
    for n in range(NL):
        pre_grad = pg_ref[n]
        for k in range(K):
            tok = block(toks, tok_piece, tok_lane, n * K + k)
            store(
                0,
                n * K + k,
                lax.dot_general(
                    tok, pre_grad, (((0,), (0,)), ((), ())), preferred_element_type=jnp.float32
                ),
            )


def terms_kernel(tab_ref, out_lane, in_lane, out_piece, in_piece, hid_ref, pg_ref, up_ref, down_ref, *refs):
    sends = refs[0:8]
    acc, packed, ups, downs, sem = refs[8:]
    core, half = tab_ref[0], tab_ref[1]
    up_copy = pltpu.make_async_copy(up_ref.at[pl.ds(half * NL, NL)], ups, sem.at[0])
    down_copy = pltpu.make_async_copy(down_ref.at[pl.ds(half * NL, NL)], downs, sem.at[1])
    down_copy.start()
    up_copy.start()
    acc[...] = jnp.zeros_like(acc)

    def place(kind, piece, lane, j, value):
        for h in range(2):
            for u in range(2):
                p = piece[(j * 2 + u) * 2 + h]
                off = pl.multiple_of(lane[j * 2 + u], HALF)
                acc[kind, p, :, pl.ds(off, HALF)] += value[
                    h * HALF : (h + 1) * HALF, u * HALF : (u + 1) * HALF
                ]

    down_copy.wait()
    for n in range(NL):
        for k in range(K):
            place(
                0,
                out_piece,
                out_lane,
                n * K + k,
                jnp.dot(hid_ref[n], downs[n, k], preferred_element_type=jnp.float32),
            )
    up_copy.wait()
    for n in range(NL):
        for k in range(K):
            place(
                1,
                in_piece,
                in_lane,
                n * K + k,
                lax.dot_general(
                    pg_ref[n], ups[n, k], (((1,), (1,)), ((), ())), preferred_element_type=jnp.float32
                ),
            )
    copies = []
    for d in (1, 2, 3, 0):
        for kind in range(2):
            for e in range(4):
                for s in range(2):
                    packed[kind, d, e, s] = acc[kind, (d * 4 + e) * 2 + s].astype(jnp.bfloat16)
        for side in range(2):
            kind = 1 - core if side else core
            copy = pltpu.make_async_copy(packed.at[kind, d], sends[side * 4 + d], sem.at[2 + side * 4 + d])
            copy.start()
            copies.append(copy)
    for copy in copies:
        copy.wait()


def any_spec():
    return pl.BlockSpec(memory_space=pl.ANY)


def vmem_spec():
    return pl.BlockSpec(memory_space=pltpu.VMEM)


def smem_spec():
    return pl.BlockSpec(memory_space=pltpu.SMEM)


def wide_sum(terms):
    total = terms[0].astype(jnp.float32)
    for term in terms[1:]:
        total = total + term.astype(jnp.float32)
    return total.astype(jnp.bfloat16)


def on_device(tokens, cotangent, up_blocks, up_index, down_blocks, down_index):
    x, core = lax.axis_index("x"), lax.axis_index("core")
    half = lax.axis_index("ylo")
    y = lax.axis_index("yhi") * 2 + half
    is0 = core == 0

    up_mine = lax.dynamic_slice_in_dim(up_index, half * NL, NL, 0)
    down_mine = lax.dynamic_slice_in_dim(down_index, half * NL, NL, 0)
    tab = jnp.stack([core, half]).astype(jnp.int32)
    dx, dy, slot, tok_lane = piece_tables(up_mine, x, y, 0, -1)
    tok_piece = (dy * 4 + dx) * 2 + slot
    dx, dy, slot, cot_lane = piece_tables(down_mine, x, y, 1, -1)
    cot_piece = (dx * 4 + dy) * 2 + slot
    dx, dy, slot, out_lane = piece_tables(down_mine, x, y, 0, 1)
    out_piece = (dx * 4 + dy) * 2 + slot
    dx, dy, slot, in_lane = piece_tables(up_mine, x, y, 1, 1)
    in_piece = (dy * 4 + dx) * 2 + slot
    tok_lane, tok_piece, cot_lane, cot_piece, out_lane, out_piece, in_lane, in_piece = [
        v.reshape(-1)
        for v in (tok_lane, tok_piece, cot_lane, cot_piece, out_lane, out_piece, in_lane, in_piece)
    ]

    with jax.named_scope("gather"):
        keep = jnp.where(is0, tokens, cotangent)
        give = jnp.where(is0, cotangent, tokens)
        own = jnp.stack([keep, permute(give, other_core)])
        line = [own] + [permute(own, first_axis(d)) for d in (1, 2, 3)]
        line = jnp.stack(line)
        mine = [line] + [permute(line, second_axis(e)) for e in (1, 2, 3)]
        theirs = [permute(part, other_core) for part in mine]

    bf16, f32 = jnp.bfloat16, jnp.float32
    hidden, pre_grad, weight_part = pl.pallas_call(
        grads_kernel,
        out_shape=(
            jax.ShapeDtypeStruct((NL, BLK, BLK), bf16),
            jax.ShapeDtypeStruct((NL, BLK, BLK), bf16),
            jax.ShapeDtypeStruct((8, 2, 2, NL * K, 16, BLK), bf16),
        ),
        in_specs=[smem_spec()] * 5 + [any_spec()] * 10,
        out_specs=(vmem_spec(), vmem_spec(), vmem_spec()),
        scratch_shapes=[
            pltpu.VMEM((4, 4, 2, HALF, WIDE), bf16),
            pltpu.VMEM((4, 4, 2, HALF, WIDE), bf16),
            pltpu.VMEM((NL, K, BLK, BLK), bf16),
            pltpu.VMEM((NL, K, BLK, BLK), bf16),
            pltpu.SemaphoreType.DMA((4,)),
        ],
        compiler_params=pltpu.CompilerParams(vmem_limit_bytes=VMEM_LIMIT),
        cost_estimate=pl.CostEstimate(
            flops=48 * 2 * BLK**3, bytes_accessed=13 << 20, transcendentals=NL * BLK * BLK * 2
        ),
        name="grads",
    )(tab, tok_lane, cot_lane, tok_piece, cot_piece, *mine, *theirs, up_blocks, down_blocks)

    with jax.named_scope("weight_sums"):
        weight_sum = lax.psum_scatter(
            weight_part.reshape(8 * 2 * 2 * NL * K * 16, BLK), "z", scatter_dimension=0, tiled=True
        ).reshape(2, 2, NL, K, 16, BLK)

    sends = pl.pallas_call(
        terms_kernel,
        out_shape=tuple(jax.ShapeDtypeStruct((4, 2, HALF, WIDE), bf16) for _ in range(8)),
        in_specs=[smem_spec()] * 5 + [vmem_spec()] * 2 + [any_spec()] * 2,
        out_specs=tuple(any_spec() for _ in range(8)),
        scratch_shapes=[
            pltpu.VMEM((2, 32, HALF, WIDE), f32),
            pltpu.VMEM((2, 4, 4, 2, HALF, WIDE), bf16),
            pltpu.VMEM((NL, K, BLK, BLK), bf16),
            pltpu.VMEM((NL, K, BLK, BLK), bf16),
            pltpu.SemaphoreType.DMA((10,)),
        ],
        compiler_params=pltpu.CompilerParams(vmem_limit_bytes=VMEM_LIMIT),
        cost_estimate=pl.CostEstimate(
            flops=24 * 2 * BLK**3, bytes_accessed=10 << 20, transcendentals=0
        ),
        name="terms",
    )(tab, out_lane, in_lane, out_piece, in_piece, hidden, pre_grad, up_blocks, down_blocks)

    with jax.named_scope("scatter"):
        kept, given = sends[:4], sends[4:]
        got = {d: permute(given[d], other_core) for d in (1, 2, 3, 0)}
        line = [kept[0], got[0]]
        for d in (1, 2, 3):
            line.append(permute(wide_sum([kept[d], got[d]]), first_axis(d)))
        line = wide_sum(line)
        final = [line[0]] + [permute(line[e], second_axis(e)) for e in (1, 2, 3)]
        final = wide_sum(final)
        last = permute(final[1], other_core)
        output = jnp.where(is0, final[0], last)
        input_grad = jnp.where(is0, last, final[0])

    with jax.named_scope("weight_halves"):
        stay = jnp.where(half == 0, weight_sum[0], weight_sum[1])
        leave = jnp.where(half == 0, weight_sum[1], weight_sum[0])
        come = permute(leave, other_half)
        low = jnp.where(half == 0, stay, come)
        high = jnp.where(half == 0, come, stay)
        both = jnp.concatenate([low, high], axis=1)
    return output, input_grad, both[0], both[1]


def solution(mesh):
    fine = Mesh(mesh.devices.reshape(2, 8, 4, 2, 2), AXES)
    dp, tensor = ("ylo", "z"), ("x", "yhi", "core")
    in_specs = (
        P(dp, tensor),
        P(dp, tensor),
        P(tensor, None, None, None),
        P(tensor, None),
        P(tensor, None, None, None),
        P(tensor, None),
    )
    out_specs = (
        P(dp, tensor),
        P(dp, tensor),
        P(tensor, None, dp, None),
        P(tensor, None, dp, None),
    )
    return jax.shard_map(
        on_device, mesh=fine, in_specs=in_specs, out_specs=out_specs, check_vma=False
    )
```

```python
import jax
import jax.numpy as jnp
from jax import lax
from jax.experimental import pallas as pl
from jax.experimental.pallas import tpu as pltpu
from jax.sharding import Mesh, PartitionSpec as P

BLK = 256
HALF = 128
WIDE = 384
K = 4
NH = 6
NB = NH * K
AXES = ("ylo", "z", "x", "yhi", "core")
VMEM_LIMIT = 40 * 1024 * 1024
BF16, F32 = jnp.bfloat16, jnp.float32


def device_id(x, y, z, c):
    return ((y % 2) * 8 + z) * 16 + x * 4 + (y // 2) * 2 + c


def permute(value, target):
    pairs = []
    for x in range(4):
        for y in range(4):
            for z in range(8):
                for c in range(2):
                    tx, ty, tz, tc = target(x, y, z, c)
                    pairs.append((device_id(x, y, z, c), device_id(tx % 4, ty % 4, tz % 8, tc)))
    return lax.ppermute(value, AXES, pairs)


def other_core(x, y, z, c):
    return x, y, z, 1 - c


def ahead_z(x, y, z, c):
    return x, y, (z + 1 if c == 0 else z - 1), c


def back_z(x, y, z, c):
    return x, y, (z - 1 if c == 0 else z + 1), c


def gather_first(step):
    return lambda x, y, z, c: (x + step, y, z, c) if c == 0 else (x, y + step, z, c)


def gather_second(step):
    return lambda x, y, z, c: (x, y + step, z, c) if c == 0 else (x + step, y, z, c)


def along_x(step):
    return lambda x, y, z, c: (x + step, y, z, c)


def across_y(x, y, z, c):
    return x, y + 2, z, c


def place():
    return [lax.axis_index(a) for a in AXES]


def unit_owner(unit):
    return (unit * 43) >> 7


def gathered_quarter(all_ref, kind, unit, token_half, x, y, core):
    t = unit_owner(unit)
    lane = (unit - 3 * t) * HALF
    c = t & 1
    dx = (x - (t >> 2)) & 3
    dy = (y - ((t & 2) + token_half)) & 3
    first = jnp.where(c == 0, dx, dy)
    second = jnp.where(c == 0, dy, dx)
    return all_ref[kind, c ^ core, second, first, :, pl.ds(pl.multiple_of(lane, HALF), HALF)]


def gathered_block(all_ref, kind, b, x, y, core):
    rows = []
    for h in range(2):
        cols = [gathered_quarter(all_ref, kind, 2 * b + u, h, x, y, core) for u in range(2)]
        rows.append(jnp.concatenate(cols, axis=1))
    return jnp.concatenate(rows, axis=0)


def dot(a, b, a_dim, b_dim):
    return lax.dot_general(a, b, (((a_dim,), (b_dim,)), ((), ())), preferred_element_type=F32)


def grads_kernel(up_idx, down_idx, *refs):
    parts, (up_hbm, down_hbm) = refs[0:8], refs[8:10]
    hid_ref, pg_ref, dw_ref, far_ref = refs[10:14]
    all_ref, up_ref, down_ref, pre_ref, sem = refs[14:]
    ylo, z, x, yhi, core = place()
    y = yhi * 2 + ylo

    def fetch(kind):
        for slot in range(2):
            for i, e in enumerate((0, 1, 3, 2)):
                pltpu.make_async_copy(
                    parts[4 * slot + i].at[:, kind], all_ref.at[kind, slot, e], sem.at[kind]
                ).start()

    def await_all(ref, i):
        pltpu.make_async_copy(ref, ref, sem.at[i]).wait()

    fetch(0)
    up_copy = pltpu.make_async_copy(up_hbm, up_ref, sem.at[2])
    up_copy.start()
    fetch(1)
    down_copy = pltpu.make_async_copy(down_hbm, down_ref, sem.at[3])
    down_copy.start()

    def store_rows(g, j, value):
        value = value.astype(BF16)
        for i in range(8):
            r = jnp.where(core == 0, i - z, z - i) & 7
            dw_ref[r, g, j] = value[i * 16 : i * 16 + 16]

    await_all(all_ref.at[0], 0)
    up_copy.wait()
    for n in range(NH):
        acc = jnp.zeros((BLK, BLK), F32)
        for k in range(K):
            tok = gathered_block(all_ref, 0, up_idx[n * K + k], x, y, core)
            acc += dot(tok, up_ref[n, k], 1, 0)
        pre_ref[n] = acc
        hid_ref[n] = (acc * jax.nn.sigmoid(acc)).astype(BF16)
    await_all(all_ref.at[1], 1)
    down_copy.wait()
    lanes = pl.ds(pl.multiple_of(ylo * HALF, HALF), HALF)
    for n in range(NH):
        hidden = hid_ref[n, :, lanes]
        acc = jnp.zeros((BLK, BLK), F32)
        for k in range(K):
            cot = gathered_block(all_ref, 1, down_idx[n * K + k], x, y, core)
            acc += dot(cot, down_ref[n, k], 1, 1)
            store_rows(1, n * K + k, dot(hidden, cot, 0, 0))
        pre = pre_ref[n]
        sig = jax.nn.sigmoid(pre)
        pre_grad = (acc * (sig * (1.0 + pre * (1.0 - sig)))).astype(BF16)
        pg_ref[n] = pre_grad
        for k in range(K):
            unit = 2 * up_idx[n * K + k] + ylo
            tok = jnp.concatenate(
                [gathered_quarter(all_ref, 0, unit, h, x, y, core) for h in range(2)], axis=0
            )
            store_rows(0, n * K + k, dot(tok, pre_grad, 0, 0))
    far_ref[...] = dw_ref[4]


def terms_kernel(up_idx, down_idx, hid_ref, pg_ref, up_ref, down_ref, *refs):
    keep, give, acc = refs[0:4], refs[4:6], refs[6]
    ylo, z, x, yhi, core = place()
    acc[...] = jnp.zeros_like(acc)

    def add(kind, b, value):
        for u in range(2):
            unit = 2 * b + u
            t = unit_owner(unit)
            lane = (unit - 3 * t) * HALF
            dx = ((t >> 2) - x) & 3
            dy = ((t >> 1) & 1) ^ yhi
            where = ((((t & 1) ^ core) * 4 + dx) * 2 + dy) * 2 + kind
            acc[where, :, pl.ds(pl.multiple_of(lane, HALF), HALF)] += value[
                :, u * HALF : (u + 1) * HALF
            ]

    rows = pl.ds(pl.multiple_of(ylo * HALF, HALF), HALF)
    for n in range(NH):
        hidden = hid_ref[n, rows]
        pre_grad = pg_ref[n, rows]
        for k in range(K):
            add(0, down_idx[n * K + k], dot(hidden, down_ref[n, k], 1, 0))
            add(1, up_idx[n * K + k], dot(pre_grad, up_ref[n, k], 1, 1))
    for dx in range(4):
        for dy in range(2):
            for kind in range(2):
                keep[dx][dy, kind] = acc[(dx * 2 + dy) * 2 + kind].astype(BF16)
                other = acc[((4 + dx) * 2 + dy) * 2 + kind].astype(BF16)
                give[0 if dx in (1, 2) else 1][dx // 2, dy, kind] = other


def specs(space, count):
    return [pl.BlockSpec(memory_space=space)] * count


def run(kernel, name, args, in_specs, out_shape, scratch, flops, moved):
    return pl.pallas_call(
        kernel,
        out_shape=tuple(out_shape),
        in_specs=in_specs,
        out_specs=tuple(specs(pltpu.VMEM, len(out_shape))),
        scratch_shapes=scratch,
        compiler_params=pltpu.CompilerParams(vmem_limit_bytes=VMEM_LIMIT),
        cost_estimate=pl.CostEstimate(flops=flops, bytes_accessed=moved, transcendentals=0),
        name=name,
    )(*args)


def shape(*dims, dtype=BF16):
    return jax.ShapeDtypeStruct(dims, dtype)


def wide_sum(*terms):
    total = terms[0].astype(F32)
    for term in terms[1:]:
        total = total + term.astype(F32)
    return total.astype(BF16)


def on_device(tokens, cotangent, up_blocks, up_index, down_blocks, down_index):
    up_idx, down_idx = up_index.reshape(-1), down_index.reshape(-1)

    with jax.named_scope("gather"):
        own = jnp.stack([tokens, cotangent])
        line = jnp.stack([own] + [permute(own, gather_first(d)) for d in (1, 2, 3)])
        mine = [line] + [permute(line, gather_second(e)) for e in (1, 3, 2)]
        theirs = [permute(part, other_core) for part in mine]

    piece = HALF * WIDE * 2
    matmul = 2 * BLK**3
    smem, vmem, anyw = pltpu.SMEM, pltpu.VMEM, pl.ANY
    hidden, pre_grad, parts, far = run(
        grads_kernel,
        "grads",
        (up_idx, down_idx, *mine, *theirs, up_blocks, down_blocks),
        specs(smem, 2) + specs(anyw, 10),
        [
            shape(NH, BLK, BLK),
            shape(NH, BLK, BLK),
            shape(8, 2, NB, 16, BLK),
            shape(2, NB, 16, BLK),
        ],
        [
            pltpu.VMEM((2, 2, 4, 4, HALF, WIDE), BF16),
            pltpu.VMEM((NH, K, BLK, BLK), BF16),
            pltpu.VMEM((NH, K, BLK, BLK), BF16),
            pltpu.VMEM((NH, BLK, BLK), F32),
            pltpu.SemaphoreType.DMA((4,)),
        ],
        72 * matmul,
        128 * piece,
    )
    with jax.named_scope("weight_sums"):
        ahead = permute(far, ahead_z)

    *keep, give_a, give_b = run(
        terms_kernel,
        "terms",
        (up_idx, down_idx, hidden, pre_grad, up_blocks, down_blocks),
        specs(smem, 2) + specs(vmem, 4),
        [shape(2, 2, HALF, WIDE)] * 4 + [shape(2, 2, 2, HALF, WIDE)] * 2,
        [pltpu.VMEM((32, HALF, WIDE), F32)],
        24 * matmul,
        96 * piece,
    )
    tie = lax.optimization_barrier
    with jax.named_scope("scatter"):
        got_a, got_b = permute(give_a, other_core), permute(give_b, other_core)
        sums = [wide_sum(keep[dx], got) for dx, got in ((1, got_a[0]), (2, got_a[1]), (3, got_b[1]))]
        ahead = wide_sum(parts[3], ahead)
        *sums, ahead, back = tie((*sums, ahead, parts[5]))
    with jax.named_scope("weight_sums"):
        ahead, back = permute(ahead, ahead_z), permute(back, back_z)
    with jax.named_scope("scatter"):
        sent = [permute(total, along_x(dx)) for dx, total in zip((1, 2, 3), sums)]
    with jax.named_scope("weight_sums"):
        ahead, back = tie((wide_sum(parts[2], ahead), wide_sum(parts[6], back)))
        *sent, _, _ = tie((*sent, ahead, back))
        ahead, back = permute(ahead, ahead_z), permute(back, back_z)
    with jax.named_scope("scatter"):
        line_sum = wide_sum(keep[0], got_b[0], *sent)
        across = permute(line_sum[1], across_y)
    with jax.named_scope("weight_sums"):
        ahead, back = tie((wide_sum(parts[1], ahead), wide_sum(parts[7], back)))
        across, _, _ = tie((across, ahead, back))
        ahead, back = permute(ahead, ahead_z), permute(back, back_z)
        weight_grads = wide_sum(parts[0], ahead, back)
    with jax.named_scope("scatter"):
        final = wide_sum(line_sum[0], across)

    rows = (NH, K, 16, BLK)
    return final[0], final[1], weight_grads[0].reshape(rows), weight_grads[1].reshape(rows)


def solution(mesh):
    fine = Mesh(mesh.devices.reshape(2, 8, 4, 2, 2), AXES)
    dp, tensor = ("ylo", "z"), ("x", "yhi", "core")
    in_specs = (
        P(dp, tensor),
        P(dp, tensor),
        P(tensor, None, None, None),
        P(tensor, None),
        P(tensor, None, None, None),
        P(tensor, None),
    )
    out_specs = (
        P(dp, tensor),
        P(dp, tensor),
        P(tensor, None, dp, None),
        P(tensor, None, dp, None),
    )
    return jax.shard_map(
        on_device, mesh=fine, in_specs=in_specs, out_specs=out_specs, check_vma=False
    )
```

```python
import jax
import jax.numpy as jnp
from jax import lax
from jax.experimental import pallas as pl
from jax.experimental.pallas import tpu as pltpu
from jax.sharding import Mesh, PartitionSpec as P

BLK = 256
HALF = 128
WIDE = 384
K = 4
NH = 6
NB = NH * K
AXES = ("ylo", "z", "x", "yhi", "core")
VMEM_LIMIT = 40 * 1024 * 1024
BF16, F32 = jnp.bfloat16, jnp.float32


def device_id(x, y, z, c):
    return ((y % 2) * 8 + z) * 16 + x * 4 + (y // 2) * 2 + c


def permute(value, target):
    pairs = []
    for x in range(4):
        for y in range(4):
            for z in range(8):
                for c in range(2):
                    tx, ty, tz, tc = target(x, y, z, c)
                    pairs.append((device_id(x, y, z, c), device_id(tx % 4, ty % 4, tz % 8, tc)))
    return lax.ppermute(value, AXES, pairs)


def other_core(x, y, z, c):
    return x, y, z, 1 - c


def ahead_z(x, y, z, c):
    return x, y, (z + 1 if c == 0 else z - 1), c


def back_z(x, y, z, c):
    return x, y, (z - 1 if c == 0 else z + 1), c


def gather_first(step):
    return lambda x, y, z, c: (x + step, y, z, c) if c == 0 else (x, y + step, z, c)


def gather_second(step):
    return lambda x, y, z, c: (x, y + step, z, c) if c == 0 else (x + step, y, z, c)


def along_x(step):
    return lambda x, y, z, c: (x + step, y, z, c)


def across_y(x, y, z, c):
    return x, y + 2, z, c


def place():
    return [lax.axis_index(a) for a in AXES]


def unit_owner(unit):
    return (unit * 43) >> 7


def gathered_quarter(all_ref, kind, unit, token_half, x, y, core):
    t = unit_owner(unit)
    lane = (unit - 3 * t) * HALF
    c = t & 1
    dx = (x - (t >> 2)) & 3
    dy = (y - ((t & 2) + token_half)) & 3
    first = jnp.where(c == 0, dx, dy)
    second = jnp.where(c == 0, dy, dx)
    return all_ref[kind, c ^ core, second, first, :, pl.ds(pl.multiple_of(lane, HALF), HALF)]


def gathered_block(all_ref, kind, b, x, y, core):
    rows = []
    for h in range(2):
        cols = [gathered_quarter(all_ref, kind, 2 * b + u, h, x, y, core) for u in range(2)]
        rows.append(jnp.concatenate(cols, axis=1))
    return jnp.concatenate(rows, axis=0)


def dot(a, b, a_dim, b_dim):
    return lax.dot_general(a, b, (((a_dim,), (b_dim,)), ((), ())), preferred_element_type=F32)


def grads_kernel(index, *refs):
    parts, (up_hbm, down_hbm) = refs[0:8], refs[8:10]
    dw_ref, far_ref, keep, give = *refs[10:12], refs[12:16], refs[16:18]
    hid_ref, acc_ref, all_ref, up_ref, down_ref, pre_ref, sem = refs[18:]
    ylo, z, x, yhi, core = place()
    y = yhi * 2 + ylo

    def fetch(kind):
        for slot in range(2):
            for i, e in enumerate((0, 1, 3, 2)):
                pltpu.make_async_copy(
                    parts[4 * slot + i].at[:, kind], all_ref.at[kind, slot, e], sem.at[kind]
                ).start()

    def await_all(ref, i):
        pltpu.make_async_copy(ref, ref, sem.at[i]).wait()

    fetch(0)
    up_copy = pltpu.make_async_copy(up_hbm, up_ref, sem.at[2])
    up_copy.start()
    fetch(1)
    down_copy = pltpu.make_async_copy(down_hbm, down_ref, sem.at[3])
    down_copy.start()

    def store_rows(g, j, value):
        value = value.astype(BF16)
        for i in range(8):
            r = jnp.where(core == 0, i - z, z - i) & 7
            dw_ref[r, g, j] = value[i * 16 : i * 16 + 16]

    def add(kind, b, value):
        for u in range(2):
            unit = 2 * b + u
            t = unit_owner(unit)
            lane = (unit - 3 * t) * HALF
            dx = ((t >> 2) - x) & 3
            dy = ((t >> 1) & 1) ^ yhi
            where = ((((t & 1) ^ core) * 4 + dx) * 2 + dy) * 2 + kind
            acc_ref[where, :, pl.ds(pl.multiple_of(lane, HALF), HALF)] += value[
                :, u * HALF : (u + 1) * HALF
            ]

    acc_ref[...] = jnp.zeros_like(acc_ref)
    own = pl.ds(pl.multiple_of(ylo * HALF, HALF), HALF)
    await_all(all_ref.at[0], 0)
    up_copy.wait()
    for n in range(NH):
        acc = jnp.zeros((BLK, BLK), F32)
        for k in range(K):
            tok = gathered_block(all_ref, 0, index[0, k, n], x, y, core)
            acc += dot(tok, up_ref[n, k], 1, 0)
        pre_ref[n] = acc
        hid_ref[n] = (acc * jax.nn.sigmoid(acc)).astype(BF16)
    await_all(all_ref.at[1], 1)
    down_copy.wait()
    for n in range(NH):
        hidden, my_hidden = hid_ref[n, :, own], hid_ref[n, own]
        acc = jnp.zeros((BLK, BLK), F32)
        for k in range(K):
            cot = gathered_block(all_ref, 1, index[1, k, n], x, y, core)
            acc += dot(cot, down_ref[n, k], 1, 1)
            store_rows(1, n * K + k, dot(hidden, cot, 0, 0))
            add(0, index[1, k, n], dot(my_hidden, down_ref[n, k], 1, 0))
        pre = pre_ref[n]
        sig = jax.nn.sigmoid(pre)
        pre_grad = (acc * (sig * (1.0 + pre * (1.0 - sig)))).astype(BF16)
        hid_ref[n] = pre_grad
        my_grad = hid_ref[n, own]
        toks = []
        for k in range(K):
            unit = 2 * index[0, k, n] + ylo
            halves = [gathered_quarter(all_ref, 0, unit, h, x, y, core) for h in range(2)]
            toks.append(jnp.concatenate(halves, axis=0))
            add(1, index[0, k, n], dot(my_grad, up_ref[n, k], 1, 1))
        grads = dot(jnp.concatenate(toks, axis=1), pre_grad, 0, 0)
        for k in range(K):
            store_rows(0, n * K + k, grads[k * HALF : (k + 1) * HALF])
    far_ref[...] = dw_ref[4]
    for dx in range(4):
        for dy in range(2):
            for kind in range(2):
                keep[dx][dy, kind] = acc_ref[(dx * 2 + dy) * 2 + kind].astype(BF16)
                other = acc_ref[((4 + dx) * 2 + dy) * 2 + kind].astype(BF16)
                give[0 if dx in (1, 2) else 1][dx // 2, dy, kind] = other


def specs(space, count):
    return [pl.BlockSpec(memory_space=space)] * count


def run(kernel, name, args, in_specs, out_shape, scratch, flops, moved):
    return pl.pallas_call(
        kernel,
        out_shape=tuple(out_shape),
        in_specs=in_specs,
        out_specs=tuple(specs(pltpu.VMEM, len(out_shape))),
        scratch_shapes=scratch,
        compiler_params=pltpu.CompilerParams(vmem_limit_bytes=VMEM_LIMIT),
        cost_estimate=pl.CostEstimate(flops=flops, bytes_accessed=moved, transcendentals=0),
        name=name,
    )(*args)


def shape(*dims, dtype=BF16):
    return jax.ShapeDtypeStruct(dims, dtype)


def wide_sum(*terms):
    total = terms[0].astype(F32)
    for term in terms[1:]:
        total = total + term.astype(F32)
    return total.astype(BF16)


def on_device(tokens, cotangent, up_blocks, up_index, down_blocks, down_index):

    tie = lax.optimization_barrier
    with jax.named_scope("gather"):
        own = jnp.stack([tokens, cotangent])
        line = [permute(own, gather_first(d)) for d in (3, 1, 2)]
        *line, up_index, down_index = tie((*line, up_index, down_index))
        index = jnp.stack([up_index.T, down_index.T])
        line = jnp.stack([own, line[1], line[2], line[0]])
        mine = [line] + [permute(line, gather_second(e)) for e in (1, 3, 2)]
        theirs = [permute(part, other_core) for part in mine]

    piece = HALF * WIDE * 2
    matmul = 2 * BLK**3
    smem, vmem, anyw = pltpu.SMEM, pltpu.VMEM, pl.ANY
    parts, far, *rest = run(
        grads_kernel,
        "grads",
        (index, *mine, *theirs, up_blocks, down_blocks),
        specs(smem, 1) + specs(anyw, 10),
        [shape(8, 2, NB, 16, BLK)]
        + [shape(2, NB, 16, BLK)]
        + [shape(2, 2, HALF, WIDE)] * 4
        + [shape(2, 2, 2, HALF, WIDE)] * 2,
        [
            pltpu.VMEM((NH, BLK, BLK), BF16),
            pltpu.VMEM((32, HALF, WIDE), F32),
            pltpu.VMEM((2, 2, 4, 4, HALF, WIDE), BF16),
            pltpu.VMEM((NH, K, BLK, BLK), BF16),
            pltpu.VMEM((NH, K, BLK, BLK), BF16),
            pltpu.VMEM((NH, BLK, BLK), F32),
            pltpu.SemaphoreType.DMA((4,)),
        ],
        96 * matmul,
        128 * piece,
    )
    keep, (give_a, give_b) = rest[:4], rest[4:]
    ahead = permute(far, ahead_z)
    got_a, got_b = permute(give_a, other_core), permute(give_b, other_core)
    sums = [wide_sum(keep[dx], got) for dx, got in ((1, got_a[0]), (2, got_a[1]), (3, got_b[1]))]
    *sums, ahead, back = tie((*sums, wide_sum(parts[3], ahead), parts[5]))
    ahead, back = permute(ahead, ahead_z), permute(back, back_z)
    sent = [permute(total, along_x(dx)) for dx, total in zip((1, 2, 3), sums)]
    ahead, back = tie((wide_sum(parts[2], ahead), wide_sum(parts[6], back)))
    *sent, _, _ = tie((*sent, ahead, back))
    ahead, back = permute(ahead, ahead_z), permute(back, back_z)
    line_sum = wide_sum(keep[0], got_b[0], *sent)
    across = permute(line_sum[1], across_y)
    ahead, back = tie((wide_sum(parts[1], ahead), wide_sum(parts[7], back)))
    across, _, _ = tie((across, ahead, back))
    ahead, back = permute(ahead, ahead_z), permute(back, back_z)
    final = wide_sum(line_sum[0], across)
    weight_grads = wide_sum(parts[0], ahead, back)

    rows = (NH, K, 16, BLK)
    return final[0], final[1], weight_grads[0].reshape(rows), weight_grads[1].reshape(rows)


def solution(mesh):
    fine = Mesh(mesh.devices.reshape(2, 8, 4, 2, 2), AXES)
    dp, tensor = ("ylo", "z"), ("x", "yhi", "core")
    in_specs = (
        P(dp, tensor),
        P(dp, tensor),
        P(tensor, None, None, None),
        P(tensor, None),
        P(tensor, None, None, None),
        P(tensor, None),
    )
    out_specs = (
        P(dp, tensor),
        P(dp, tensor),
        P(tensor, None, dp, None),
        P(tensor, None, dp, None),
    )
    return jax.shard_map(
        on_device, mesh=fine, in_specs=in_specs, out_specs=out_specs, check_vma=False
    )
```

```python
import jax
import jax.numpy as jnp
from jax import lax
from jax.experimental import pallas as pl
from jax.experimental.pallas import tpu as pltpu
from jax.sharding import Mesh, PartitionSpec as P

BLK = 256
HALF = 128
WIDE = 384
K = 4
NH = 6
NB = NH * K
AXES = ("ylo", "z", "x", "yhi", "core")
VMEM_LIMIT = 40 * 1024 * 1024
BF16, F32 = jnp.bfloat16, jnp.float32


def device_id(x, y, z, c):
    return ((y % 2) * 8 + z) * 16 + x * 4 + (y // 2) * 2 + c


def permute(value, target):
    pairs = []
    for x in range(4):
        for y in range(4):
            for z in range(8):
                for c in range(2):
                    tx, ty, tz, tc = target(x, y, z, c)
                    pairs.append((device_id(x, y, z, c), device_id(tx % 4, ty % 4, tz % 8, tc)))
    return lax.ppermute(value, AXES, pairs)


def other_core(x, y, z, c):
    return x, y, z, 1 - c


def ahead_z(x, y, z, c):
    return x, y, (z + 1 if c == 0 else z - 1), c


def back_z(x, y, z, c):
    return x, y, (z - 1 if c == 0 else z + 1), c


def gather_first(step):
    return lambda x, y, z, c: (x + step, y, z, c) if c == 0 else (x, y + step, z, c)


def gather_second(step):
    return lambda x, y, z, c: (x, y + step, z, c) if c == 0 else (x + step, y, z, c)


def along_x(step):
    return lambda x, y, z, c: (x + step, y, z, c)


def across_y(x, y, z, c):
    return x, y + 2, z, c


def place():
    return [lax.axis_index(a) for a in AXES]


def unit_owner(unit):
    return (unit * 43) >> 7


def gathered_quarter(all_ref, kind, unit, token_half, x, y, core):
    t = unit_owner(unit)
    lane = (unit - 3 * t) * HALF
    c = t & 1
    dx = (x - (t >> 2)) & 3
    dy = (y - ((t & 2) + token_half)) & 3
    first = jnp.where(c == 0, dx, dy)
    second = jnp.where(c == 0, dy, dx)
    return all_ref[c ^ core, second, first, kind, :, pl.ds(pl.multiple_of(lane, HALF), HALF)]


def gathered_block(all_ref, kind, b, x, y, core):
    rows = []
    for h in range(2):
        cols = [gathered_quarter(all_ref, kind, 2 * b + u, h, x, y, core) for u in range(2)]
        rows.append(jnp.concatenate(cols, axis=1))
    return jnp.concatenate(rows, axis=0)


def dot(a, b, a_dim, b_dim):
    return lax.dot_general(a, b, (((a_dim,), (b_dim,)), ((), ())), preferred_element_type=F32)


def grads_kernel(index, *refs):
    parts, (up_hbm, down_hbm) = refs[0:8], refs[8:10]
    dw_ref, far_ref, keep, give = *refs[10:12], refs[12:16], refs[16:18]
    hid_ref, acc_ref, all_ref, up_ref, down_ref, pre_ref, sem = refs[18:]
    ylo, z, x, yhi, core = place()
    y = yhi * 2 + ylo

    for slot in range(2):
        for i, e in enumerate((0, 1, 3, 2)):
            pltpu.make_async_copy(parts[4 * slot + i], all_ref.at[slot, e], sem.at[0]).start()

    def await_all(ref, i):
        pltpu.make_async_copy(ref, ref, sem.at[i]).wait()

    up_copy = pltpu.make_async_copy(up_hbm, up_ref, sem.at[2])
    up_copy.start()
    down_copy = pltpu.make_async_copy(down_hbm, down_ref, sem.at[3])
    down_copy.start()

    def store_rows(g, j, value):
        value = value.astype(BF16)
        for i in range(8):
            r = jnp.where(core == 0, i - z, z - i) & 7
            dw_ref[r, g, j] = value[i * 16 : i * 16 + 16]

    def add(kind, b, value):
        for u in range(2):
            unit = 2 * b + u
            t = unit_owner(unit)
            lane = (unit - 3 * t) * HALF
            dx = ((t >> 2) - x) & 3
            dy = ((t >> 1) & 1) ^ yhi
            where = ((((t & 1) ^ core) * 4 + dx) * 2 + dy) * 2 + kind
            acc_ref[where, :, pl.ds(pl.multiple_of(lane, HALF), HALF)] += value[
                :, u * HALF : (u + 1) * HALF
            ]

    acc_ref[...] = jnp.zeros_like(acc_ref)
    own = pl.ds(pl.multiple_of(ylo * HALF, HALF), HALF)
    await_all(all_ref, 0)
    up_copy.wait()
    for n in range(NH):
        acc = jnp.zeros((BLK, BLK), F32)
        for k in range(K):
            tok = gathered_block(all_ref, 0, index[0, k, n], x, y, core)
            acc += dot(tok, up_ref[n, k], 1, 0)
        pre_ref[n] = acc
        hid_ref[n] = (acc * jax.nn.sigmoid(acc)).astype(BF16)
    down_copy.wait()
    for n in range(NH):
        hidden, my_hidden = hid_ref[n, :, own], hid_ref[n, own]
        acc = jnp.zeros((BLK, BLK), F32)
        for k in range(K):
            cot = gathered_block(all_ref, 1, index[1, k, n], x, y, core)
            acc += dot(cot, down_ref[n, k], 1, 1)
            store_rows(1, n * K + k, dot(hidden, cot, 0, 0))
            add(0, index[1, k, n], dot(my_hidden, down_ref[n, k], 1, 0))
        pre = pre_ref[n]
        sig = jax.nn.sigmoid(pre)
        pre_grad = (acc * (sig * (1.0 + pre * (1.0 - sig)))).astype(BF16)
        hid_ref[n] = pre_grad
        my_grad = hid_ref[n, own]
        toks = []
        for k in range(K):
            unit = 2 * index[0, k, n] + ylo
            halves = [gathered_quarter(all_ref, 0, unit, h, x, y, core) for h in range(2)]
            toks.append(jnp.concatenate(halves, axis=0))
            add(1, index[0, k, n], dot(my_grad, up_ref[n, k], 1, 1))
        grads = dot(jnp.concatenate(toks, axis=1), pre_grad, 0, 0)
        for k in range(K):
            store_rows(0, n * K + k, grads[k * HALF : (k + 1) * HALF])
    far_ref[...] = dw_ref[4]
    for dx in range(4):
        for dy in range(2):
            for kind in range(2):
                keep[dx][dy, kind] = acc_ref[(dx * 2 + dy) * 2 + kind].astype(BF16)
                other = acc_ref[((4 + dx) * 2 + dy) * 2 + kind].astype(BF16)
                give[0 if dx in (1, 2) else 1][dx // 2, dy, kind] = other


def specs(space, count):
    return [pl.BlockSpec(memory_space=space)] * count


def run(kernel, name, args, in_specs, out_shape, scratch, flops, moved):
    return pl.pallas_call(
        kernel,
        out_shape=tuple(out_shape),
        in_specs=in_specs,
        out_specs=tuple(specs(pltpu.VMEM, len(out_shape))),
        scratch_shapes=scratch,
        compiler_params=pltpu.CompilerParams(vmem_limit_bytes=VMEM_LIMIT),
        cost_estimate=pl.CostEstimate(flops=flops, bytes_accessed=moved, transcendentals=0),
        name=name,
    )(*args)


def shape(*dims, dtype=BF16):
    return jax.ShapeDtypeStruct(dims, dtype)


def wide_sum(*terms):
    total = terms[0].astype(F32)
    for term in terms[1:]:
        total = total + term.astype(F32)
    return total.astype(BF16)


def on_device(tokens, cotangent, up_blocks, up_index, down_blocks, down_index):

    tie = lax.optimization_barrier
    with jax.named_scope("gather"):
        own = jnp.stack([tokens, cotangent])
        line = [permute(own, gather_first(d)) for d in (3, 1, 2)]
        *line, up_index, down_index = tie((*line, up_index, down_index))
        index = jnp.stack([up_index.T, down_index.T])
        line = jnp.stack([own, line[1], line[2], line[0]])
        mine = [line] + [permute(line, gather_second(e)) for e in (1, 3, 2)]
        theirs = [permute(part, other_core) for part in mine]

    piece = HALF * WIDE * 2
    matmul = 2 * BLK**3
    smem, vmem, anyw = pltpu.SMEM, pltpu.VMEM, pl.ANY
    parts, far, *rest = run(
        grads_kernel,
        "grads",
        (index, *mine, *theirs, up_blocks, down_blocks),
        specs(smem, 1) + specs(anyw, 10),
        [shape(8, 2, NB, 16, BLK)]
        + [shape(2, NB, 16, BLK)]
        + [shape(2, 2, HALF, WIDE)] * 4
        + [shape(2, 2, 2, HALF, WIDE)] * 2,
        [
            pltpu.VMEM((NH, BLK, BLK), BF16),
            pltpu.VMEM((32, HALF, WIDE), F32),
            pltpu.VMEM((2, 4, 4, 2, HALF, WIDE), BF16),
            pltpu.VMEM((NH, K, BLK, BLK), BF16),
            pltpu.VMEM((NH, K, BLK, BLK), BF16),
            pltpu.VMEM((NH, BLK, BLK), F32),
            pltpu.SemaphoreType.DMA((4,)),
        ],
        96 * matmul,
        128 * piece,
    )
    keep, (give_a, give_b) = rest[:4], rest[4:]
    ahead = permute(far, ahead_z)
    got_a, got_b = permute(give_a, other_core), permute(give_b, other_core)
    sums = [wide_sum(keep[dx], got) for dx, got in ((1, got_a[0]), (2, got_a[1]), (3, got_b[1]))]
    ahead, back = tie((wide_sum(parts[3], ahead), parts[5]))
    *sums, _, _ = tie((*sums, ahead, back))
    ahead, back = permute(ahead, ahead_z), permute(back, back_z)
    sent = [permute(total, along_x(dx)) for dx, total in zip((1, 2, 3), sums)]
    ahead, back = tie((wide_sum(parts[2], ahead), wide_sum(parts[6], back)))
    *sent, _, _ = tie((*sent, ahead, back))
    ahead, back = permute(ahead, ahead_z), permute(back, back_z)
    line_sum = wide_sum(keep[0], got_b[0], *sent)
    across = permute(line_sum[1], across_y)
    ahead, back = tie((wide_sum(parts[1], ahead), wide_sum(parts[7], back)))
    across, _, _ = tie((across, ahead, back))
    ahead, back = permute(ahead, ahead_z), permute(back, back_z)
    final = wide_sum(line_sum[0], across)
    weight_grads = wide_sum(parts[0], ahead, back)

    rows = (NH, K, 16, BLK)
    return final[0], final[1], weight_grads[0].reshape(rows), weight_grads[1].reshape(rows)


def solution(mesh):
    fine = Mesh(mesh.devices.reshape(2, 8, 4, 2, 2), AXES)
    dp, tensor = ("ylo", "z"), ("x", "yhi", "core")
    in_specs = (
        P(dp, tensor),
        P(dp, tensor),
        P(tensor, None, None, None),
        P(tensor, None),
        P(tensor, None, None, None),
        P(tensor, None),
    )
    out_specs = (
        P(dp, tensor),
        P(dp, tensor),
        P(tensor, None, dp, None),
        P(tensor, None, dp, None),
    )
    return jax.shard_map(
        on_device, mesh=fine, in_specs=in_specs, out_specs=out_specs, check_vma=False
    )
```
